32 devices in a mesh: section: 2 (over y), expert: 16 (over z, x, core).
Axes of the slice: x: 2, y: 2, z: 4, core: 2. Of those that a mesh axis runs over, the one named last changes fastest.
Arguments:
- inputs: bfloat16 [2, 64, 4096], P(None, None, 'expert'), may hold values from -6 to 6
- expert_ids: int32 [64, 2, 2], P('expert'), may hold values from 0 to 7, all different within a row; in each aligned block of 8 rows (0 to 7, 8 to 15, ..., all dimensions but the last counted through in order) at most 2 rows name the same one
- mamba_gain: float32 [2, 4096], P('section', 'expert'), may hold values from 0.1 to 1.9
- dt_in: bfloat16 [2, 4096, 256], P('section', 'expert'), may hold values from -0.09375 to 0.09375
- dt_out: bfloat16 [2, 256, 4096], P('section', None, 'expert'), may hold values from -0.375 to 0.375
- dt_bias: float32 [2, 4096], P('section', 'expert'), may hold values from -5 to 0
- state_in: bfloat16 [2, 4096, 32], P('section', 'expert'), may hold values from -0.09375 to 0.09375
- decay_rate: float32 [2, 4096, 16], P('section', 'expert'), may hold values from 0.02 to 2
- skip_gain: float32 [2, 4096], P('section', 'expert'), may hold values from 0.5 to 1.5
- moe_gain: float32 [4096], replicated, may hold values from 0.1 to 1.9
- router: bfloat16 [4096, 8], replicated, may hold values from -0.25 to 0.25
- expert_in: bfloat16 [2, 4096, 98304], P(None, 'section', 'expert'), may hold values from -0.09375 to 0.09375
- expert_out: bfloat16 [98304, 4096], P('expert', 'section'), may hold values from -0.21875 to 0.21875
Outputs:
- layer_out: bfloat16 [2, 64, 4096], P(None, 'expert', 'section')
The draws below stay inside these ranges and needn't reach their ends.
Inputs may be any that keep to these rules, and one draw needn't show every extreme that they name: `expert_ids`: within each aligned block of 8 rows of the first two dimensions taken together, every expert is named exactly 2 times; a row names 2 different experts.
All inputs are finite; a program needn't handle non-finite values.
Results may differ from the reference program's by a relative error of at most 0.029.
Values may be sent and summed in bfloat16 or wider, within the bound.
A program may use at most 192 MiB of HBM per device.

```python
import math
import jax
import jax.numpy as jnp
import numpy as np
from jax import lax

D = 4096
STATE = 16
DT_RANK = 256
EXP = 8
TOP = 2
FF_W = 12288
MICRO = 2
TOK_DEV = 4
SEQ = 64
CAP = 2
GROUP = 2
FF_DEV = 6144
D_SECTION = 2048
N_SECTION = 2
N_EXPERT = 16


def levels(stream_key, shape, cuts, low, top_value):
    level = 1.0
    for dim, shards_of in cuts:
        steps = jax.random.uniform(jax.random.fold_in(jax.random.fold_in(stream_key, 6), dim), (shards_of,), jnp.float32, low / len(cuts), top_value / len(cuts))
        level = level * jnp.repeat(jnp.exp(steps), shape[dim] // shards_of).reshape((-1,) + (1,) * (len(shape) - 1 - dim))
    return level


def assign_block(rng, own, number, rows, number_of, top, most, skew):
    order = jax.random.permutation(rng, number_of)
    crowded, ordinary = shares(number_of, rows * top, most, skew, True), shares(number_of, rows * top, most, skew, False)
    places = jnp.arange(number_of)

    def named(sizes, rotation):
        used = int((sizes > 0).sum())
        fixed = max(1, used // 4)
        passed = fixed + (places - fixed + rotation * (used - fixed)) % max(1, number_of - fixed)
        return jnp.zeros((number_of,), jnp.int32).at[order[jnp.where(places < fixed, places, passed)]].set(jnp.asarray(sizes, jnp.int32))

    sizes = jnp.where(number % 4 == 0, named(crowded, number // 4), named(ordinary, number - number // 4 - 1))
    mixed = jax.random.permutation(jax.random.fold_in(own, 3), number_of)
    giver, receiver = mixed[0:number_of // 2 * 2:2], mixed[1:number_of // 2 * 2:2]
    slack = jnp.minimum(sizes[giver] - 1, most - sizes[receiver]) // 2
    slack = jnp.where((giver == order[0]) | (receiver == order[0]) | (sizes[receiver] == 0), 0, jnp.maximum(slack, 0))
    passed = jax.random.randint(jax.random.fold_in(own, 4), (number_of // 2,), 0, 1 << 20) % (slack + 1)
    sizes = sizes.at[giver].add(-passed).at[receiver].add(passed)
    members = jnp.searchsorted(jnp.cumsum(sizes), jnp.arange(rows * top), side="right").astype(jnp.int32)
    table = members.reshape(top, rows).T
    table = table[jax.random.permutation(jax.random.fold_in(own, 1), rows)]
    rotation = jax.random.randint(jax.random.fold_in(own, 2), (rows, 1), 0, top)
    return jnp.take_along_axis(table, (jnp.arange(top)[None, :] + rotation) % top, axis=1)


def shares(amount, total, limit, lean, full):
    weights = [(1 << 20) // math.isqrt(grade ** lean) + 1 for grade in range(1, amount + 1)]
    largest = limit if full else min(limit, max(-(-total // amount), total * weights[0] // sum(weights)))
    least = 1 if total - largest >= amount - 1 else 0
    holding, spare = [largest] + [least] * (amount - 1), total - largest - least * (amount - 1)
    while spare > 0:
        free = [i for i in range(1, amount) if holding[i] < largest] or [i for i in range(1, amount) if holding[i] < limit]
        mass, left = sum([weights[i] for i in free]), spare
        for i in free:
            more = min(limit - holding[i], max(1, left * weights[i] // mass), spare)
            holding[i] = holding[i] + more
            spare = spare - more
    return np.array(holding)


def gaussian(key, shape, scale, reach, cuts=(), kind=jnp.bfloat16):
    drawn = scale * jax.random.normal(key, shape, jnp.float32)
    if cuts:
        drawn = drawn * levels(key, shape, cuts, -0.22, 0.18)
    return jnp.clip(drawn, -reach, reach).astype(kind)


def setup_inputs(seed: int = 0) -> dict:
    arg_keys = jax.random.split(jax.random.key(seed), 14)
    inputs = gaussian(arg_keys[0], (MICRO, SEQ, D), 1.0, 6.0, ((2, 16),))
    expert_ids_keys = jax.random.split(jax.random.fold_in(arg_keys[1], 1), SEQ * MICRO // (MICRO * TOK_DEV))
    expert_ids_turns = jax.random.permutation(jax.random.fold_in(arg_keys[1], 3), SEQ * MICRO // (MICRO * TOK_DEV))
    expert_ids = jax.vmap(lambda own, number: assign_block(jax.random.fold_in(arg_keys[1], 2), own, number, MICRO * TOK_DEV, EXP, TOP, CAP, 0))(expert_ids_keys, expert_ids_turns).reshape((SEQ, MICRO, TOP))
    mamba_gain = jnp.clip(1.0 + 0.18 * jax.random.normal(arg_keys[2], (N_SECTION, D), jnp.float32), 0.1, 1.9)
    dt_in = gaussian(arg_keys[3], (N_SECTION, D, DT_RANK), D ** -0.5, 0.09375, ((0, 2), (1, 16)))
    dt_out = gaussian(arg_keys[4], (N_SECTION, DT_RANK, D), DT_RANK ** -0.5, 0.375, ((0, 2), (2, 16)))
    dt_bias = jnp.clip(-5.0 + 5.0 * jax.random.uniform(arg_keys[5], (N_SECTION, D), jnp.float32) ** levels(arg_keys[5], (N_SECTION, D), ((0, 2), (1, 16)), -0.2, 0.2), -5.0, 0.0)
    state_in = gaussian(arg_keys[6], (N_SECTION, D, 2 * STATE), D ** -0.5, 0.09375, ((0, 2), (1, 16)))
    decay_rate = jnp.clip(jnp.exp(math.log(2.0) - 4.6051702 * jax.random.uniform(arg_keys[7], (N_SECTION, D, STATE), jnp.float32) ** levels(arg_keys[7], (N_SECTION, D, STATE), ((0, 2), (1, 16)), -0.2, 0.2)), 0.02, 2.0)
    skip_gain = jnp.clip(0.5 + 1.0 * jax.random.uniform(arg_keys[8], (N_SECTION, D), jnp.float32) ** levels(arg_keys[8], (N_SECTION, D), ((0, 2), (1, 16)), -0.2, 0.2), 0.5, 1.5)
    moe_gain = jnp.clip(1.0 + 0.18 * jax.random.normal(arg_keys[9], (D,), jnp.float32), 0.1, 1.9)
    router = gaussian(arg_keys[10], (D, EXP), (D // 9) ** -0.5, 0.25)
    expert_in = gaussian(arg_keys[11], (2, D, EXP * FF_W), D ** -0.5, 0.09375, ((1, 2), (2, 16)))
    expert_out = gaussian(arg_keys[12], (EXP * FF_W, D), (FF_W // 16) ** -0.5, 0.21875, ((0, 16), (1, 2)))
    return {"inputs": inputs, "expert_ids": expert_ids, "mamba_gain": mamba_gain, "dt_in": dt_in, "dt_out": dt_out, "dt_bias": dt_bias, "state_in": state_in, "decay_rate": decay_rate, "skip_gain": skip_gain, "moe_gain": moe_gain, "router": router, "expert_in": expert_in, "expert_out": expert_out}


def normed(values, gain):
    return values * lax.rsqrt(lax.optimization_barrier(jnp.mean(values * values, axis=-1, keepdims=True)) + 1e-05) * gain

def mamba_layer(hidden_in, gain, dt_in_w, dt_out_w, bias_w, state_w, rate_w, skip_w):
    hidden_f = hidden_in.astype(jnp.float32)
    normed_u = normed(hidden_f, gain).astype(jnp.bfloat16)
    low_rank = jnp.dot(normed_u, dt_in_w, preferred_element_type=jnp.float32).astype(jnp.bfloat16)
    step_dt = jax.nn.softplus(jnp.dot(low_rank, dt_out_w, preferred_element_type=jnp.float32) + bias_w)
    both = jnp.dot(normed_u, state_w, preferred_element_type=jnp.float32)
    b_in = both[:, :STATE]
    c_out = both[:, STATE:]
    u_float = normed_u.astype(jnp.float32)

    def advance(carried, pieces):
        dt_row, u_row, b_row, c_row = pieces
        carried = jnp.exp(-dt_row[:, None] * rate_w) * carried + (dt_row * u_row)[:, None] * b_row[None, :]
        return (carried, lax.optimization_barrier(jnp.sum(carried * c_row[None, :], axis=1)))
    begin = jnp.zeros(rate_w.shape, jnp.float32)
    _, mixed = lax.scan(advance, begin, (step_dt, u_float, b_in, c_out))
    output = mixed + skip_w * u_float
    return (hidden_f + output * jax.nn.silu(u_float)).astype(jnp.bfloat16)

def reference(inputs, expert_ids, mamba_gain, dt_in, dt_out, dt_bias, state_in, decay_rate, skip_gain, moe_gain, router, expert_in, expert_out):
    finals = []
    for batch_index in range(MICRO):
        current = inputs[batch_index]
        for section_index in range(N_SECTION):
            current = mamba_layer(current, mamba_gain[section_index], dt_in[section_index], dt_out[section_index], dt_bias[section_index], state_in[section_index], decay_rate[section_index], skip_gain[section_index])
        finals.append(current)
    hidden = jnp.stack(finals, axis=1)
    hidden_f = hidden.astype(jnp.float32)
    normed_u = normed(hidden_f, moe_gain).astype(jnp.bfloat16)
    logits = jnp.dot(normed_u.reshape(-1, D), router, preferred_element_type=jnp.float32)
    probs = jax.nn.softmax(logits, axis=-1).reshape(SEQ, MICRO, EXP)
    picked = jnp.take_along_axis(probs, expert_ids, axis=2)
    weights = picked / lax.optimization_barrier(jnp.sum(picked, axis=2, keepdims=True))
    block_rows = TOK_DEV * MICRO * TOP
    flat_ids = expert_ids.reshape(N_EXPERT, block_rows)
    onehot = (flat_ids[:, :, None] == jnp.arange(EXP, dtype=jnp.int32)[None, None, :]).astype(jnp.int32)
    ranks = lax.optimization_barrier(jnp.sum((jnp.cumsum(onehot, axis=1) - onehot) * onehot, axis=2))
    slots = (flat_ids * CAP + ranks).astype(jnp.int32)
    place = (slots[:, None, :] == jnp.arange(EXP * CAP, dtype=jnp.int32)[None, :, None]).astype(jnp.float32)
    repeated = jnp.repeat(normed_u.reshape(N_EXPERT, TOK_DEV * MICRO, D), TOP, axis=1).astype(jnp.float32)
    packed = jnp.einsum('bst,btd->bsd', place, repeated).astype(jnp.bfloat16)
    by_expert = packed.reshape(N_EXPERT, EXP, CAP, D).transpose(1, 0, 2, 3).reshape(EXP, N_EXPERT * CAP, D)

    def one_expert(index):
        rows_e = lax.dynamic_index_in_dim(by_expert, index, 0, keepdims=False)
        w_first = lax.dynamic_slice_in_dim(expert_in, index * FF_W, FF_W, axis=2)
        w_second = lax.dynamic_slice_in_dim(expert_out, index * FF_W, FF_W, axis=0)
        rows_split = rows_e.reshape(-1, N_SECTION, D_SECTION).astype(jnp.float32)
        w_split = w_first.reshape(2, N_SECTION, D_SECTION, FF_W).astype(jnp.float32)
        parts = jnp.einsum('rsk,gskf->sgrf', rows_split, w_split).astype(jnp.bfloat16)
        pre = lax.optimization_barrier(jnp.sum(parts.astype(jnp.float32), axis=0))
        units = (jax.nn.silu(pre[0]) * pre[1]).astype(jnp.bfloat16)
        down_parts = jnp.einsum('rjf,jfd->jrd', units.reshape(-1, GROUP, FF_DEV).astype(jnp.float32), w_second.reshape(GROUP, FF_DEV, D).astype(jnp.float32)).astype(jnp.bfloat16)
        return lax.optimization_barrier(jnp.sum(down_parts.astype(jnp.float32), axis=0))
    results = lax.map(one_expert, jnp.arange(EXP, dtype=jnp.int32))
    back = results.reshape(EXP, N_EXPERT, CAP, D).transpose(1, 0, 2, 3).reshape(N_EXPERT, EXP * CAP, D)
    chosen = jnp.take_along_axis(back, slots[:, :, None], axis=1)
    chosen = chosen.reshape(SEQ, MICRO, TOP, D)
    routed = lax.optimization_barrier(jnp.sum(chosen * weights[:, :, :, None], axis=2))
    mixed_out = (hidden_f + routed).astype(jnp.bfloat16)
    return mixed_out.transpose(1, 0, 2)
```

```python
import functools

import jax
import jax.numpy as jnp
from jax import lax
from jax.experimental import pallas as pl
from jax.experimental.pallas import tpu as pltpu
from jax.sharding import PartitionSpec as P


def passed_along(array, axis, by):
    peers = lax.axis_size(axis)
    pairs = [(i, i + by) for i in range(peers) if 0 <= i + by < peers]
    return lax.ppermute(array, axis, pairs)


def from_root(array, axis, root):
    mine = lax.axis_index(axis) == root
    return lax.psum(jnp.where(mine, array, jnp.zeros_like(array)), axis)


def normed(values, gain):
    return values * lax.rsqrt(jnp.mean(values * values, axis=-1, keepdims=True) + 1e-05) * gain


def scan_rows(step_dt, u_float, b_in, c_out, rate_w):
    row_count = step_dt.shape[0]
    blocks = row_count // 16
    pieces = (
        step_dt.reshape(blocks, 16, -1),
        u_float.reshape(blocks, 16, -1),
        b_in.reshape(blocks, 16, -1),
        c_out.reshape(blocks, 16, -1),
    )

    def advance(carried, block_pieces):
        dt_block, u_block, b_block, c_block = block_pieces
        emitted = []
        for index in range(16):
            carried = (
                jnp.exp(-dt_block[index][:, None] * rate_w) * carried
                + (dt_block[index] * u_block[index])[:, None] * b_block[index][None, :]
            )
            emitted.append(jnp.sum(carried * c_block[index][None, :], axis=1))
        return (carried, jnp.stack(emitted))

    begin = jnp.zeros(rate_w.shape, jnp.float32)
    _, mixed = lax.scan(advance, begin, pieces)
    return mixed.reshape(row_count, -1)


def mamba_layer(hidden_in, gain, dt_in_w, dt_out_w, bias_w, state_w, rate_w, skip_w):
    state_size = rate_w.shape[1]
    full_width = hidden_in.shape[1] * lax.axis_size("expert")
    hidden_f = hidden_in.astype(jnp.float32)
    squares = lax.psum(jnp.sum(hidden_f * hidden_f, axis=1), "expert")
    scale = lax.rsqrt(squares / full_width + 1e-05)
    normed_u = (hidden_f * scale[:, None] * gain).astype(jnp.bfloat16)
    low_part = jnp.dot(normed_u, dt_in_w, preferred_element_type=jnp.float32)
    state_part = jnp.dot(normed_u, state_w, preferred_element_type=jnp.float32)
    low_sum, state_sum = lax.psum((low_part, state_part), "expert")
    low_rank = low_sum.astype(jnp.bfloat16)
    step_dt = jax.nn.softplus(
        jnp.dot(low_rank, dt_out_w, preferred_element_type=jnp.float32) + bias_w
    )
    b_in = state_sum[:, :state_size]
    c_out = state_sum[:, state_size:]
    u_float = normed_u.astype(jnp.float32)
    mixed = scan_rows(step_dt, u_float, b_in, c_out, rate_w)
    output = mixed + skip_w * u_float
    return (hidden_f + output * jax.nn.silu(u_float)).astype(jnp.bfloat16)


def moe_layer(hidden, ids, gain, router_w, in_w, out_w):
    batches, tok_rows, full_width = hidden.shape
    experts = router_w.shape[1]
    top_count = ids.shape[2]
    devices = lax.axis_size("expert")
    group = devices // experts
    slice_width = in_w.shape[1]
    section_here = lax.axis_index("section")
    capacity = tok_rows * batches * top_count // experts
    ordered = hidden.transpose(1, 0, 2).reshape(-1, full_width)
    hidden_f = ordered.astype(jnp.float32)
    normed_u = normed(hidden_f, gain).astype(jnp.bfloat16)
    probs = jax.nn.softmax(jnp.dot(normed_u, router_w, preferred_element_type=jnp.float32), axis=-1)
    id_rows = ids.reshape(-1, top_count)
    picked = jnp.take_along_axis(probs, id_rows, axis=1)
    weights = picked / jnp.sum(picked, axis=1, keepdims=True)
    flat_ids = ids.reshape(-1)
    onehot = (flat_ids[:, None] == jnp.arange(experts, dtype=jnp.int32)[None, :]).astype(jnp.int32)
    ranks = jnp.sum((jnp.cumsum(onehot, axis=0) - onehot) * onehot, axis=1)
    slots = flat_ids * capacity + ranks
    place = (slots[None, :] == jnp.arange(experts * capacity, dtype=jnp.int32)[:, None]).astype(
        jnp.bfloat16
    )
    repeated = jnp.repeat(normed_u, top_count, axis=0)
    packed = jnp.dot(place, repeated, preferred_element_type=jnp.float32).astype(jnp.bfloat16)
    my_features = lax.dynamic_slice_in_dim(packed, section_here * slice_width, slice_width, 1)
    outgoing = jnp.broadcast_to(
        my_features.reshape(experts, 1, capacity, slice_width),
        (experts, group, capacity, slice_width),
    ).reshape(devices, capacity, slice_width)
    arrived = lax.all_to_all(outgoing, "expert", split_axis=0, concat_axis=0, tiled=True)
    rows_in = arrived.reshape(-1, slice_width)
    gate_part = jnp.dot(rows_in, in_w[0], preferred_element_type=jnp.float32)
    up_part = jnp.dot(rows_in, in_w[1], preferred_element_type=jnp.float32)
    gate_sum, up_sum = (
        lax.psum(gate_part.astype(jnp.bfloat16), "section").astype(jnp.float32),
        lax.psum(up_part.astype(jnp.bfloat16), "section").astype(jnp.float32),
    )
    units = (jax.nn.silu(gate_sum) * up_sum).astype(jnp.bfloat16)
    produced = jnp.dot(units, out_w, preferred_element_type=jnp.float32).astype(jnp.bfloat16)
    finished = lax.all_to_all(
        produced.reshape(devices, capacity, slice_width),
        "expert",
        split_axis=0,
        concat_axis=0,
        tiled=True,
    )
    summed = jnp.sum(
        finished.reshape(experts, group, capacity, slice_width).astype(jnp.float32), axis=1
    )
    lookup = summed.reshape(experts * capacity, slice_width)
    chosen = lookup[slots].reshape(-1, top_count, slice_width)
    routed = jnp.sum(chosen * weights[:, :, None], axis=1)
    residual = lax.dynamic_slice_in_dim(hidden_f, section_here * slice_width, slice_width, 1)
    mixed_out = (residual + routed).astype(jnp.bfloat16)
    return mixed_out.reshape(tok_rows, batches, slice_width).transpose(1, 0, 2)


def shards(
    inputs,
    expert_ids,
    mamba_gain,
    dt_in,
    dt_out,
    dt_bias,
    state_in,
    decay_rate,
    skip_gain,
    moe_gain,
    router,
    expert_in,
    expert_out,
):
    sections = lax.axis_size("section")
    section_here = lax.axis_index("section")
    batches = inputs.shape[0]

    def tick(moment, carried):
        received, results = carried
        batch_index = moment - section_here
        active = jnp.logical_and(batch_index >= 0, batch_index < batches)
        clipped = jnp.clip(batch_index, 0, batches - 1)
        first_rows = lax.dynamic_index_in_dim(inputs, clipped, 0, keepdims=False)
        current = jnp.where(section_here == 0, first_rows, received)
        produced = mamba_layer(
            current,
            mamba_gain[0],
            dt_in[0],
            dt_out[0],
            dt_bias[0],
            state_in[0],
            decay_rate[0],
            skip_gain[0],
        )
        updated = lax.dynamic_update_index_in_dim(results, produced, clipped, 0)
        results = jnp.where(active, updated, results)
        passed = passed_along(produced, "section", 1)
        return (passed, results)

    begin = (jnp.zeros(inputs.shape[1:], jnp.bfloat16), jnp.zeros(inputs.shape, jnp.bfloat16))
    _, results = lax.fori_loop(0, batches + sections - 1, tick, begin)
    finals = from_root(results, "section", sections - 1)
    hidden = lax.all_to_all(finals, "expert", split_axis=1, concat_axis=2, tiled=True)
    return moe_layer(hidden, expert_ids, moe_gain, router, expert_in, expert_out)


MESH = pl.DeviceIdType.MESH
STEP_COLUMNS = 512
IN_SLOTS = 9
OUT_SLOTS = 7
WIDE = 384


def iota(shape, dim):
    return lax.broadcasted_iota(jnp.int32, shape, dim)


def kernel(
    inputs, ids, gain, dt_in, dt_out, bias, state_w, rate, skip, moe_gain, router, w_in, w_out,
    out,
    win, wout, part, rs_buf, summed, ag_buf, third, step_ref, du_ref, mixed_ref, b_ref, c_ref,
    own, relay, slot_buf, stat_buf, xsend, xrow, rsend, resid, parts, theirs, units, acc, ret, back,
    in_sem, out_sem, rs_send, rs_recv, ag_send, ag_recv, relay_send, relay_recv,
    slot_send, slot_recv, stat_send, stat_recv, x_send, x_recv, r_send, r_recv,
    p_send, p_recv, u_send, u_recv, b_send, b_recv,
):
    f32, bf16 = jnp.float32, jnp.bfloat16
    peers = lax.axis_size("expert")
    sec, me = lax.axis_index("section"), lax.axis_index("expert")
    partner = (1 - sec, me)
    batches, seq, chans = inputs.shape
    rows = batches * seq
    chips = peers // 2
    full = chans * peers
    steps = w_in.shape[2] // STEP_COLUMNS
    half = steps // 2

    def remote(src, dst, ssem, rsem, device):
        return pltpu.make_async_remote_copy(
            src_ref=src, dst_ref=dst, send_sem=ssem, recv_sem=rsem,
            device_id=device, device_id_type=MESH,
        )

    def in_copy(n):
        chunk = lax.rem(n + (1 - sec) * half, steps)
        slot = lax.rem(n, IN_SLOTS)
        at = pl.multiple_of(chunk * STEP_COLUMNS, STEP_COLUMNS)
        return pltpu.make_async_copy(
            w_in.at[:, :, pl.ds(at, STEP_COLUMNS)], win.at[slot], in_sem.at[slot]
        )

    def out_copy(n):
        chunk = lax.rem(n + sec * half, steps)
        slot = lax.rem(n, OUT_SLOTS)
        at = pl.multiple_of(chunk * STEP_COLUMNS, STEP_COLUMNS)
        return pltpu.make_async_copy(
            w_out.at[pl.ds(at, STEP_COLUMNS), :], wout.at[slot], out_sem.at[slot]
        )

    def loop(first, last, body):
        def step(n, none):
            body(n)
            return none
        lax.fori_loop(first, last, step, 0)

    barrier = pltpu.get_barrier_semaphore()
    total = 2 * peers

    def greet(n):
        line = lax.rem(sec * peers + me + n, total)
        pl.semaphore_signal(
            barrier, inc=1, device_id=(line // peers, lax.rem(line, peers)), device_id_type=MESH
        )

    loop(1, total, greet)
    loop(0, IN_SLOTS, lambda n: in_copy(n).start())
    loop(0, OUT_SLOTS, lambda n: out_copy(n).start())

    lane, sub = iota((16, 128), 1), iota((16, 128), 0)
    across, down = jnp.full((16, 128), -1, jnp.int32), jnp.full((16, 128), -2, jnp.int32)
    for j in range(16):
        value = ids[j // 4, (j // 2) % 2, j % 2]
        across = jnp.where(lane == j, value, across)
        down = jnp.where(sub == j, value, down)
    earlier = jnp.where((across == down) & (sub < lane), 1.0, 0.0)
    rank = jnp.sum(earlier, axis=0, keepdims=True)
    slot_row = across[:1].astype(f32) * 2.0 + rank
    slot_buf[me] = jnp.broadcast_to(slot_row, (8, 128))
    pl.semaphore_wait(barrier, total - 1)

    def slot_copy(n):
        return remote(
            slot_buf.at[me], slot_buf.at[me], slot_send.at[n], slot_recv.at[me],
            (sec, lax.rem(me + n, peers)),
        )

    loop(1, peers, lambda n: slot_copy(n).start())

    @pl.when(sec == 1)
    def _():
        remote(own, relay, relay_send, relay_recv, partner).wait_recv()

    first = inputs[...].reshape(rows, chans)
    h = jnp.where(sec == 0, first.astype(f32), relay[...].astype(f32))
    scaled = h * gain[...]
    scaled_b = scaled.astype(bf16)
    squares = jnp.sum(h * h, axis=1, keepdims=True)
    high = squares.astype(bf16).astype(f32)
    lanes = iota((rows, 128), 1)
    third[...] = jnp.where(lanes == 32, high, jnp.where(lanes == 33, squares - high, 0.0))
    third[:, :32] = jnp.dot(scaled_b, state_w[0], preferred_element_type=f32)
    low = jnp.dot(scaled_b, dt_in[0], preferred_element_type=f32)
    part[:, :256] = low.astype(bf16)
    part[:, 256:] = third[...].astype(bf16)

    def rs_copy(n):
        chip = lax.rem(me // 2 + n, chips)
        at = pl.multiple_of(chip * 16, 16)
        return remote(
            part.at[pl.ds(at, 16)], rs_buf.at[me], rs_send.at[n], rs_recv.at[me], (sec, chip * 2)
        )

    odd = lax.rem(me, 2) == 1

    @pl.when(odd)
    def _():
        rs_copy(0).start()

    loop(1, chips, lambda n: rs_copy(n).start())

    def ag_copy(n):
        at = pl.multiple_of(me // 2 * 16, 16)
        return remote(
            summed, ag_buf.at[pl.ds(at, 16)], ag_send.at[n], ag_recv.at[me // 2],
            (sec, lax.rem(me + n, peers)),
        )

    def rs_arrived(source):
        return remote(part.at[pl.ds(0, 16)], rs_buf.at[source], rs_send.at[0], rs_recv.at[source], (sec, me))

    @pl.when(jnp.logical_not(odd))
    def _():
        at = pl.multiple_of(me // 2 * 16, 16)
        rs_buf[me] = part[pl.ds(at, 16), :]
        loop(1, peers, lambda n: rs_arrived(lax.rem(me + n, peers)).wait_recv())
        whole = jnp.sum(rs_buf[...].astype(f32), axis=0)
        square = whole[:, 288:289] + whole[:, 289:290]
        scale = lax.rsqrt(square / full + 1e-05)
        scale_high = scale.astype(bf16).astype(f32)
        lane3 = iota((16, WIDE), 1)
        result = jnp.where(
            lane3 == 288, scale_high, jnp.where(lane3 == 289, scale - scale_high, whole * scale)
        )
        summed[...] = result.astype(bf16)
        ag_buf[pl.ds(at, 16), :] = summed[...]
        loop(1, peers, lambda n: ag_copy(n).start())

    def ag_arrived(chip):
        at = pl.multiple_of(chip * 16, 16)
        return remote(summed, ag_buf.at[pl.ds(at, 16)], ag_send.at[0], ag_recv.at[chip], (sec, me))

    @pl.when(odd)
    def _():
        ag_arrived(me // 2).wait_recv()

    loop(1, chips, lambda n: ag_arrived(lax.rem(me // 2 + n, chips)).wait_recv())

    tail = ag_buf[:, 256:]
    tail_f = tail.astype(f32)
    scale = tail_f[:, 32:33] + tail_f[:, 33:34]
    u = (scaled_of(h, scale, gain[...])).astype(bf16).astype(f32)
    step_pre = jnp.dot(ag_buf[:, :256], dt_out[0], preferred_element_type=f32) + bias[...]
    step_dt = jnp.maximum(step_pre, 0.0) + jnp.log1p(jnp.exp(-jnp.abs(step_pre)))
    step_ref[...] = step_dt
    du_ref[...] = step_dt * u
    spread = jnp.where(iota((rows * 16, rows), 0) >> 4 == iota((rows * 16, rows), 1), 1.0, 0.0)
    repeated = jnp.dot(spread.astype(bf16), tail, preferred_element_type=f32)
    state_lane = iota((rows * 16, 128), 1)
    state_row = iota((rows * 16, 128), 0) & 15
    ones = jnp.ones((128, 128), bf16)
    b_ref[...] = jnp.dot(
        jnp.where(state_lane == state_row, repeated, 0.0).astype(bf16), ones,
        preferred_element_type=f32,
    )
    c_ref[...] = jnp.dot(
        jnp.where(state_lane == state_row + 16, repeated, 0.0).astype(bf16), ones,
        preferred_element_type=f32,
    )
    negative = -jnp.transpose(rate[0])

    def advance(t, states):
        after = []
        for m in range(batches):
            row = m * seq + t
            at = pl.multiple_of(row * 16, 16)
            b_in, c_out = b_ref[pl.ds(at, 16), :], c_ref[pl.ds(at, 16), :]
            b_in = jnp.concatenate([b_in] * (chans // 128), axis=1)
            c_out = jnp.concatenate([c_out] * (chans // 128), axis=1)
            state = (
                jnp.exp(step_ref[pl.ds(row, 1), :] * negative) * states[m]
                + du_ref[pl.ds(row, 1), :] * b_in
            )
            mixed_ref[pl.ds(row, 1), :] = jnp.sum(state * c_out, axis=0, keepdims=True)
            after.append(state)
        return tuple(after)

    lax.fori_loop(
        0, seq, advance, tuple(jnp.zeros((16, chans), f32) for _ in range(batches)), unroll=4
    )
    mixed = mixed_ref[...] + skip[...] * u
    own[...] = (h + mixed * (u / (1.0 + jnp.exp(-u)))).astype(bf16)
    relay_copy = remote(own, relay, relay_send, relay_recv, partner)
    relay_copy.start()

    def slot_arrived(n):
        source = lax.rem(me + n, peers)
        remote(
            slot_buf.at[source], slot_buf.at[source], slot_send.at[0], slot_recv.at[source], (sec, me)
        ).wait_recv()

    loop(1, peers, slot_arrived)
    slot_table = jnp.concatenate([slot_buf[n, :1, :] for n in range(peers)], axis=0).astype(bf16)
    token = iota((1, 128), 1)
    position, batch = token & (seq - 1), token // seq
    j_row, token_at = iota((128, 128), 0), iota((128, 128), 1)
    flat_first = ((token_at & 3) * 2 + token_at // seq) * 2
    block_mask = iota((peers, 128), 0) == (iota((peers, 128), 1) & (seq - 1)) >> 2
    slots = []
    for k in range(2):
        pick = jnp.where(j_row == flat_first + k, 1.0, 0.0).astype(bf16)
        picked = jnp.dot(slot_table, pick, preferred_element_type=f32)
        slots.append(jnp.sum(jnp.where(block_mask, picked, 0.0), axis=0, keepdims=True))

    def placed(count, expert):
        q, r = iota((count, 128), 0), iota((count, 128), 1)
        wanted = ((expert + (q >> 5)) * 2 + (q & 1)).astype(f32)
        same = ((q >> 1) & (peers - 1)) == (r & (seq - 1)) >> 2
        return same & ((slots[0] == wanted) | (slots[1] == wanted))

    place_all = jnp.where(placed(16 * peers, 0), 1.0, 0.0).astype(bf16)
    q, r = iota((rows, rows), 0), iota((rows, rows), 1)
    regroup = jnp.where(
        r == ((q >> 2) & 1) * seq + (q >> 3) * 4 + (q & 3), 1.0, 0.0
    ).astype(bf16)

    @pl.when(sec == 0)
    def _():
        relay_copy.wait_recv()

    final = jnp.where(sec == 0, relay[...].astype(f32), own[...].astype(f32))
    own_at = pl.multiple_of(me * chans, chans)
    final_scaled = (final * moe_gain[:, pl.ds(own_at, chans)]).astype(bf16)
    squares = jnp.sum(final * final, axis=1, keepdims=True)
    third[...] = jnp.where(lanes == 8, squares, 0.0)
    third[:, :8] = jnp.dot(
        final_scaled, router[pl.ds(own_at, chans), :], preferred_element_type=f32
    )
    stat_buf[me] = jnp.transpose(third[...])[:16]

    def stat_copy(n):
        return remote(
            stat_buf.at[me], stat_buf.at[me], stat_send.at[n], stat_recv.at[me],
            (sec, lax.rem(me + n, peers)),
        )

    xsend[...] = jnp.dot(place_all, final_scaled, preferred_element_type=f32).astype(bf16)
    rsend[...] = jnp.dot(regroup, final.astype(bf16), preferred_element_type=f32)
    to_section = me // chips
    column = pl.multiple_of(lax.rem(me, chips) * chans, chans)

    def x_copy(n):
        chip = lax.rem(me // 2 + n, chips)
        at = pl.multiple_of(chip * 32, 32)
        return remote(
            xsend.at[pl.ds(at, 32)], xrow.at[:, pl.ds(column, chans)], x_send.at[n],
            x_recv.at[lax.rem(me, chips)], (to_section, chip * 2 + sec),
        )

    def r_copy(n):
        block = lax.rem(me // 2 + n, chips) * 2 + sec
        at = pl.multiple_of(block * 8, 8)
        return remote(
            rsend.at[pl.ds(at, 8)], resid.at[:, pl.ds(column, chans)], r_send.at[n],
            r_recv.at[lax.rem(me, chips)], (to_section, block),
        )

    itself = (to_section == sec) & (lax.rem(me, 2) == sec)

    @pl.when(itself)
    def _():
        xrow[:, pl.ds(column, chans)] = xsend[pl.ds(pl.multiple_of(me // 2 * 32, 32), 32), :]
        resid[:, pl.ds(column, chans)] = rsend[pl.ds(pl.multiple_of(me * 8, 8), 8), :]

    @pl.when(jnp.logical_not(itself))
    def _():
        x_copy(0).start()

    loop(1, chips, lambda n: x_copy(n).start())
    loop(1, peers, lambda n: stat_copy(n).start())

    @pl.when(jnp.logical_not(itself))
    def _():
        r_copy(0).start()

    loop(1, chips, lambda n: r_copy(n).start())

    def x_arrived(j):
        @pl.when(jnp.logical_not(itself & (j == lax.rem(me, chips))))
        def _():
            at = pl.multiple_of(j * chans, chans)
            remote(
                xsend.at[pl.ds(0, 32)], xrow.at[:, pl.ds(at, chans)], x_send.at[0], x_recv.at[j],
                (sec, me),
            ).wait_recv()

    def r_arrived(j):
        @pl.when(jnp.logical_not(itself & (j == lax.rem(me, chips))))
        def _():
            at = pl.multiple_of(j * chans, chans)
            remote(
                rsend.at[pl.ds(0, 8)], resid.at[:, pl.ds(at, chans)], r_send.at[0], r_recv.at[j],
                (sec, me),
            ).wait_recv()

    def stat_arrived(n):
        source = lax.rem(me + n, peers)
        remote(
            stat_buf.at[source], stat_buf.at[source], stat_send.at[0], stat_recv.at[source], (sec, me)
        ).wait_recv()

    loop(1, peers, stat_arrived)
    stats = jnp.sum(stat_buf[...], axis=0)
    token_scale = lax.rsqrt(stats[8:9] / full + 1e-05)
    logits = stats[:8] * token_scale
    exps = jnp.exp(logits - jnp.max(logits, axis=0, keepdims=True))
    probs = exps / jnp.sum(exps, axis=0, keepdims=True)
    expert_row = iota((8, 128), 0)
    chosen = [
        jnp.sum(
            jnp.where(expert_row == slots[k].astype(jnp.int32) >> 1, probs, 0.0),
            axis=0, keepdims=True,
        )
        for k in range(2)
    ]
    both = chosen[0] + chosen[1]
    weights = [chosen[k] / both for k in range(2)]
    row_scale = jnp.sum(
        jnp.where(placed(32, me // 2), token_scale, 0.0), axis=1, keepdims=True
    )
    loop(0, chips, x_arrived)

    def part_copy(n):
        return remote(parts.at[n], theirs.at[n], p_send.at[n], p_recv.at[n], partner)

    def first_matmuls(n):
        slot = lax.rem(n, IN_SLOTS)
        in_copy(n).wait()
        for g in range(2):
            product = jnp.dot(xrow[...], win[slot, g], preferred_element_type=f32)
            parts[n, g] = (product * row_scale).astype(bf16)

        @pl.when(n < half)
        def _():
            part_copy(n).start()

        @pl.when(n + IN_SLOTS < steps)
        def _():
            in_copy(n + IN_SLOTS).start()

    loop(0, steps, first_matmuls)

    def unit_copy(k):
        return remote(units.at[k], units.at[half + k], u_send.at[k], u_recv.at[k], partner)

    def down_matmul(n):
        slot = lax.rem(n, OUT_SLOTS)
        out_copy(n).wait()
        acc[...] += jnp.dot(units[n], wout[slot], preferred_element_type=f32)

        @pl.when(n + OUT_SLOTS < steps)
        def _():
            out_copy(n + OUT_SLOTS).start()

    acc[...] = jnp.zeros_like(acc)

    def own_units(k):
        part_copy(k).wait_recv()
        gate = parts[half + k, 0].astype(f32) + theirs[k, 0].astype(f32)
        up = parts[half + k, 1].astype(f32) + theirs[k, 1].astype(f32)
        units[k] = (gate / (1.0 + jnp.exp(-gate)) * up).astype(bf16)
        unit_copy(k).start()
        down_matmul(k)

    loop(0, half, own_units)

    def other_units(k):
        unit_copy(k).wait_recv()
        down_matmul(half + k)

    loop(0, half, other_units)

    pieces = acc.shape[1] // chans
    stacked = jnp.concatenate(
        [acc[:, f * chans:(f + 1) * chans] for f in range(pieces)], axis=0
    ).astype(bf16)
    count = 32 * pieces
    q, z = iota((count, count), 0), iota((count, count), 1)
    order = jnp.where(
        z == (q & 7) * 32 + (q >> 4) * 2 + ((q >> 3) & 1), 1.0, 0.0
    ).astype(bf16)
    ret[...] = jnp.dot(order, stacked, preferred_element_type=f32).astype(bf16)

    def back_copy(n):
        block = lax.rem(me + n, peers)
        to = pl.multiple_of(block * 16, 16)
        at = pl.multiple_of(me * 16, 16)
        return remote(
            ret.at[pl.ds(to, 16)], back.at[pl.ds(at, 16)], b_send.at[n], b_recv.at[me], (sec, block)
        )

    loop(1, peers, lambda n: back_copy(n).start())
    mine_at = pl.multiple_of(me * 16, 16)
    back[pl.ds(mine_at, 16), :] = ret[pl.ds(mine_at, 16), :]

    tok, lane64 = iota((64, 128), 0) & 7, iota((64, 128), 1)
    here = lane64 == (tok >> 2) * seq + me * 4 + (tok & 3)
    mix_row, mix_lane = iota((64, 256), 0), iota((64, 256), 1)
    slot_of = ((mix_lane >> 5) * 2 + ((mix_lane >> 3) & 1)).astype(f32)
    aligned = (mix_row >> 3) == (mix_lane & 7)
    mix = jnp.zeros((64, 256), f32)
    for k in range(2):
        weight = jnp.sum(jnp.where(here, weights[k], 0.0), axis=1, keepdims=True)
        slot = jnp.sum(jnp.where(here, slots[k], 0.0), axis=1, keepdims=True)
        mix = mix + jnp.where(aligned & (slot == slot_of), weight, 0.0)
    mix_high = mix.astype(bf16)
    mix_low = (mix - mix_high.astype(f32)).astype(bf16)
    loop(0, chips, r_arrived)

    def back_arrived(n):
        source = lax.rem(me + n, peers)
        at = pl.multiple_of(source * 16, 16)
        remote(
            ret.at[pl.ds(0, 16)], back.at[pl.ds(at, 16)], b_send.at[0], b_recv.at[source], (sec, me)
        ).wait_recv()

    loop(1, peers, back_arrived)
    routed = jnp.dot(mix_high, back[...], preferred_element_type=f32) + jnp.dot(
        mix_low, back[...], preferred_element_type=f32
    )
    for f in range(pieces):
        columns = slice(f * chans, (f + 1) * chans)
        value = (resid[:, columns] + routed[f * 8:(f + 1) * 8]).astype(bf16)
        out[0, :, columns] = value[:4]
        out[1, :, columns] = value[4:]

    @pl.when(odd)
    def _():
        rs_copy(0).wait_send()

    loop(1, chips, lambda n: rs_copy(n).wait_send())

    @pl.when(jnp.logical_not(odd))
    def _():
        loop(1, peers, lambda n: ag_copy(n).wait_send())

    @pl.when(jnp.logical_not(itself))
    def _():
        x_copy(0).wait_send()
        r_copy(0).wait_send()

    def x_left(n):
        x_copy(n).wait_send()
        r_copy(n).wait_send()

    loop(1, chips, x_left)

    def rest_left(n):
        slot_copy(n).wait_send()
        stat_copy(n).wait_send()
        back_copy(n).wait_send()

    loop(1, peers, rest_left)

    def halves_left(k):
        part_copy(k).wait_send()
        unit_copy(k).wait_send()

    loop(0, half, halves_left)
    relay_copy.wait_send()


def scaled_of(h, scale, gain):
    return h * scale * gain


def fused(
    inputs, expert_ids, mamba_gain, dt_in, dt_out, dt_bias, state_in, decay_rate, skip_gain,
    moe_gain, router, expert_in, expert_out,
):
    f32, bf16 = jnp.float32, jnp.bfloat16
    peers = lax.axis_size("expert")
    batches, seq, chans = inputs.shape
    rows = batches * seq
    depth, columns = expert_in.shape[1:]
    steps = columns // STEP_COLUMNS
    half = steps // 2
    chips = peers // 2
    vmem = pl.BlockSpec(memory_space=pltpu.VMEM)
    smem = pl.BlockSpec(memory_space=pltpu.SMEM)
    hbm = pl.BlockSpec(memory_space=pl.ANY)
    dma = pltpu.SemaphoreType.DMA
    scratch = [
        pltpu.VMEM((IN_SLOTS, 2, depth, STEP_COLUMNS), bf16),
        pltpu.VMEM((OUT_SLOTS, STEP_COLUMNS, depth), bf16),
        pltpu.VMEM((rows, WIDE), bf16),
        pltpu.VMEM((peers, 16, WIDE), bf16),
        pltpu.VMEM((16, WIDE), bf16),
        pltpu.VMEM((rows, WIDE), bf16),
        pltpu.VMEM((rows, 128), f32),
        pltpu.VMEM((rows, chans), f32),
        pltpu.VMEM((rows, chans), f32),
        pltpu.VMEM((rows, chans), f32),
        pltpu.VMEM((rows * 16, 128), f32),
        pltpu.VMEM((rows * 16, 128), f32),
        pltpu.VMEM((rows, chans), bf16),
        pltpu.VMEM((rows, chans), bf16),
        pltpu.VMEM((peers, 8, 128), f32),
        pltpu.VMEM((peers, 16, 128), f32),
        pltpu.VMEM((16 * peers, chans), bf16),
        pltpu.VMEM((32, depth), bf16),
        pltpu.VMEM((rows, chans), f32),
        pltpu.VMEM((8, depth), f32),
        pltpu.VMEM((steps, 2, 32, STEP_COLUMNS), bf16),
        pltpu.VMEM((half, 2, 32, STEP_COLUMNS), bf16),
        pltpu.VMEM((steps, 32, STEP_COLUMNS), bf16),
        pltpu.VMEM((32, depth), f32),
        pltpu.VMEM((16 * peers, chans), bf16),
        pltpu.VMEM((16 * peers, chans), bf16),
        dma((IN_SLOTS,)), dma((OUT_SLOTS,)),
        dma((chips,)), dma((peers,)), dma((peers,)), dma((chips,)), dma, dma,
        dma((peers,)), dma((peers,)), dma((peers,)), dma((peers,)),
        dma((chips,)), dma((chips,)), dma((chips,)), dma((chips,)),
        dma((half,)), dma((half,)), dma((half,)), dma((half,)),
        dma((peers,)), dma((peers,)),
    ]
    return pl.pallas_call(
        kernel,
        out_shape=jax.ShapeDtypeStruct((batches, seq // peers, depth), bf16),
        in_specs=[vmem, smem] + [vmem] * 9 + [hbm, hbm],
        out_specs=vmem,
        scratch_shapes=scratch,
        compiler_params=pltpu.CompilerParams(
            collective_id=0, has_side_effects=True, vmem_limit_bytes=62 << 20
        ),
    )(
        inputs, expert_ids, mamba_gain, dt_in, dt_out, dt_bias, state_in, decay_rate, skip_gain,
        moe_gain.reshape(1, -1), router, expert_in, expert_out,
    )


def fits(mesh):
    return mesh.shape["section"] == 2 and mesh.shape["expert"] == 16


def solution(mesh):
    placed = (
        P(None, None, "expert"),
        P("expert", None, None),
        P("section", "expert"),
        P("section", "expert", None),
        P("section", None, "expert"),
        P("section", "expert"),
        P("section", "expert", None),
        P("section", "expert", None),
        P("section", "expert"),
        P(),
        P(),
        P(None, "section", "expert"),
        P("expert", "section"),
    )
    body = fused if fits(mesh) else shards
    return jax.shard_map(
        body, mesh=mesh, in_specs=placed, out_specs=P(None, "expert", "section"), check_vma=False
    )
```

```python
import functools

import jax
import jax.numpy as jnp
from jax import lax
from jax.experimental import pallas as pl
from jax.experimental.pallas import tpu as pltpu
from jax.sharding import PartitionSpec as P


def passed_along(array, axis, by):
    peers = lax.axis_size(axis)
    pairs = [(i, i + by) for i in range(peers) if 0 <= i + by < peers]
    return lax.ppermute(array, axis, pairs)


def from_root(array, axis, root):
    mine = lax.axis_index(axis) == root
    return lax.psum(jnp.where(mine, array, jnp.zeros_like(array)), axis)


def normed(values, gain):
    return values * lax.rsqrt(jnp.mean(values * values, axis=-1, keepdims=True) + 1e-05) * gain


def scan_rows(step_dt, u_float, b_in, c_out, rate_w):
    row_count = step_dt.shape[0]
    blocks = row_count // 16
    pieces = (
        step_dt.reshape(blocks, 16, -1),
        u_float.reshape(blocks, 16, -1),
        b_in.reshape(blocks, 16, -1),
        c_out.reshape(blocks, 16, -1),
    )

    def advance(carried, block_pieces):
        dt_block, u_block, b_block, c_block = block_pieces
        emitted = []
        for index in range(16):
            carried = (
                jnp.exp(-dt_block[index][:, None] * rate_w) * carried
                + (dt_block[index] * u_block[index])[:, None] * b_block[index][None, :]
            )
            emitted.append(jnp.sum(carried * c_block[index][None, :], axis=1))
        return (carried, jnp.stack(emitted))

    begin = jnp.zeros(rate_w.shape, jnp.float32)
    _, mixed = lax.scan(advance, begin, pieces)
    return mixed.reshape(row_count, -1)


def mamba_layer(hidden_in, gain, dt_in_w, dt_out_w, bias_w, state_w, rate_w, skip_w):
    state_size = rate_w.shape[1]
    full_width = hidden_in.shape[1] * lax.axis_size("expert")
    hidden_f = hidden_in.astype(jnp.float32)
    squares = lax.psum(jnp.sum(hidden_f * hidden_f, axis=1), "expert")
    scale = lax.rsqrt(squares / full_width + 1e-05)
    normed_u = (hidden_f * scale[:, None] * gain).astype(jnp.bfloat16)
    low_part = jnp.dot(normed_u, dt_in_w, preferred_element_type=jnp.float32)
    state_part = jnp.dot(normed_u, state_w, preferred_element_type=jnp.float32)
    low_sum, state_sum = lax.psum((low_part, state_part), "expert")
    low_rank = low_sum.astype(jnp.bfloat16)
    step_dt = jax.nn.softplus(
        jnp.dot(low_rank, dt_out_w, preferred_element_type=jnp.float32) + bias_w
    )
    b_in = state_sum[:, :state_size]
    c_out = state_sum[:, state_size:]
    u_float = normed_u.astype(jnp.float32)
    mixed = scan_rows(step_dt, u_float, b_in, c_out, rate_w)
    output = mixed + skip_w * u_float
    return (hidden_f + output * jax.nn.silu(u_float)).astype(jnp.bfloat16)


def moe_layer(hidden, ids, gain, router_w, in_w, out_w):
    batches, tok_rows, full_width = hidden.shape
    experts = router_w.shape[1]
    top_count = ids.shape[2]
    devices = lax.axis_size("expert")
    group = devices // experts
    slice_width = in_w.shape[1]
    section_here = lax.axis_index("section")
    capacity = tok_rows * batches * top_count // experts
    ordered = hidden.transpose(1, 0, 2).reshape(-1, full_width)
    hidden_f = ordered.astype(jnp.float32)
    normed_u = normed(hidden_f, gain).astype(jnp.bfloat16)
    probs = jax.nn.softmax(jnp.dot(normed_u, router_w, preferred_element_type=jnp.float32), axis=-1)
    id_rows = ids.reshape(-1, top_count)
    picked = jnp.take_along_axis(probs, id_rows, axis=1)
    weights = picked / jnp.sum(picked, axis=1, keepdims=True)
    flat_ids = ids.reshape(-1)
    onehot = (flat_ids[:, None] == jnp.arange(experts, dtype=jnp.int32)[None, :]).astype(jnp.int32)
    ranks = jnp.sum((jnp.cumsum(onehot, axis=0) - onehot) * onehot, axis=1)
    slots = flat_ids * capacity + ranks
    place = (slots[None, :] == jnp.arange(experts * capacity, dtype=jnp.int32)[:, None]).astype(
        jnp.bfloat16
    )
    repeated = jnp.repeat(normed_u, top_count, axis=0)
    packed = jnp.dot(place, repeated, preferred_element_type=jnp.float32).astype(jnp.bfloat16)
    my_features = lax.dynamic_slice_in_dim(packed, section_here * slice_width, slice_width, 1)
    outgoing = jnp.broadcast_to(
        my_features.reshape(experts, 1, capacity, slice_width),
        (experts, group, capacity, slice_width),
    ).reshape(devices, capacity, slice_width)
    arrived = lax.all_to_all(outgoing, "expert", split_axis=0, concat_axis=0, tiled=True)
    rows_in = arrived.reshape(-1, slice_width)
    gate_part = jnp.dot(rows_in, in_w[0], preferred_element_type=jnp.float32)
    up_part = jnp.dot(rows_in, in_w[1], preferred_element_type=jnp.float32)
    gate_sum, up_sum = (
        lax.psum(gate_part.astype(jnp.bfloat16), "section").astype(jnp.float32),
        lax.psum(up_part.astype(jnp.bfloat16), "section").astype(jnp.float32),
    )
    units = (jax.nn.silu(gate_sum) * up_sum).astype(jnp.bfloat16)
    produced = jnp.dot(units, out_w, preferred_element_type=jnp.float32).astype(jnp.bfloat16)
    finished = lax.all_to_all(
        produced.reshape(devices, capacity, slice_width),
        "expert",
        split_axis=0,
        concat_axis=0,
        tiled=True,
    )
    summed = jnp.sum(
        finished.reshape(experts, group, capacity, slice_width).astype(jnp.float32), axis=1
    )
    lookup = summed.reshape(experts * capacity, slice_width)
    chosen = lookup[slots].reshape(-1, top_count, slice_width)
    routed = jnp.sum(chosen * weights[:, :, None], axis=1)
    residual = lax.dynamic_slice_in_dim(hidden_f, section_here * slice_width, slice_width, 1)
    mixed_out = (residual + routed).astype(jnp.bfloat16)
    return mixed_out.reshape(tok_rows, batches, slice_width).transpose(1, 0, 2)


def shards(
    inputs,
    expert_ids,
    mamba_gain,
    dt_in,
    dt_out,
    dt_bias,
    state_in,
    decay_rate,
    skip_gain,
    moe_gain,
    router,
    expert_in,
    expert_out,
):
    sections = lax.axis_size("section")
    section_here = lax.axis_index("section")
    batches = inputs.shape[0]

    def tick(moment, carried):
        received, results = carried
        batch_index = moment - section_here
        active = jnp.logical_and(batch_index >= 0, batch_index < batches)
        clipped = jnp.clip(batch_index, 0, batches - 1)
        first_rows = lax.dynamic_index_in_dim(inputs, clipped, 0, keepdims=False)
        current = jnp.where(section_here == 0, first_rows, received)
        produced = mamba_layer(
            current,
            mamba_gain[0],
            dt_in[0],
            dt_out[0],
            dt_bias[0],
            state_in[0],
            decay_rate[0],
            skip_gain[0],
        )
        updated = lax.dynamic_update_index_in_dim(results, produced, clipped, 0)
        results = jnp.where(active, updated, results)
        passed = passed_along(produced, "section", 1)
        return (passed, results)

    begin = (jnp.zeros(inputs.shape[1:], jnp.bfloat16), jnp.zeros(inputs.shape, jnp.bfloat16))
    _, results = lax.fori_loop(0, batches + sections - 1, tick, begin)
    finals = from_root(results, "section", sections - 1)
    hidden = lax.all_to_all(finals, "expert", split_axis=1, concat_axis=2, tiled=True)
    return moe_layer(hidden, expert_ids, moe_gain, router, expert_in, expert_out)


MESH = pl.DeviceIdType.MESH
STEP_COLUMNS = 512
IN_SLOTS = 9
OUT_SLOTS = 7
WIDE = 384


def iota(shape, dim):
    return lax.broadcasted_iota(jnp.int32, shape, dim)


def kernel(
    inputs, ids, gain, dt_in, dt_out, bias, state_w, rate, skip, moe_gain, router, w_in, w_out,
    out,
    win, wout, part, rs_buf, summed, ag_buf, third, h_ref, step_ref, du_ref, mixed_ref, b_ref, c_ref,
    own, relay, slot_buf, stat_buf, xsend, xrow, rsend, resid, parts, theirs, units, acc, ret, back,
    in_sem, out_sem, rs_send, rs_recv, ag_send, ag_recv, relay_send, relay_recv,
    slot_send, slot_recv, stat_send, stat_recv, x_send, x_recv, r_send, r_recv,
    p_send, p_recv, u_send, u_recv, b_send, b_recv,
):
    f32, bf16 = jnp.float32, jnp.bfloat16
    peers = lax.axis_size("expert")
    sec, me = lax.axis_index("section"), lax.axis_index("expert")
    partner = (1 - sec, me)
    across_last = (((1,), (1,)), ((), ()))
    batches, seq, chans = inputs.shape
    rows = batches * seq
    chips = peers // 2
    full = chans * peers
    steps = w_in.shape[2] // STEP_COLUMNS
    half = steps // 2

    def remote(src, dst, ssem, rsem, device):
        return pltpu.make_async_remote_copy(
            src_ref=src, dst_ref=dst, send_sem=ssem, recv_sem=rsem,
            device_id=device, device_id_type=MESH,
        )

    def in_copy(n):
        chunk = lax.rem(n + (1 - sec) * half, steps)
        slot = lax.rem(n, IN_SLOTS)
        at = pl.multiple_of(chunk * STEP_COLUMNS, STEP_COLUMNS)
        return pltpu.make_async_copy(
            w_in.at[:, :, pl.ds(at, STEP_COLUMNS)], win.at[slot], in_sem.at[slot]
        )

    def out_copy(n):
        chunk = lax.rem(n + sec * half, steps)
        slot = lax.rem(n, OUT_SLOTS)
        at = pl.multiple_of(chunk * STEP_COLUMNS, STEP_COLUMNS)
        return pltpu.make_async_copy(
            w_out.at[pl.ds(at, STEP_COLUMNS), :], wout.at[slot], out_sem.at[slot]
        )

    def loop(first, last, body):
        def step(n, none):
            body(n)
            return none
        lax.fori_loop(first, last, step, 0)

    barrier = pltpu.get_barrier_semaphore()
    total = 2 * peers

    def greet(n):
        line = lax.rem(sec * peers + me + n, total)
        pl.semaphore_signal(
            barrier, inc=1, device_id=(line // peers, lax.rem(line, peers)), device_id_type=MESH
        )

    loop(1, total, greet)
    loop(0, IN_SLOTS, lambda n: in_copy(n).start())
    loop(0, OUT_SLOTS, lambda n: out_copy(n).start())

    lane, sub = iota((16, 128), 1), iota((16, 128), 0)
    across, down = jnp.full((16, 128), -1, jnp.int32), jnp.full((16, 128), -2, jnp.int32)
    for j in range(16):
        value = ids[(j // 2) % 2, j % 2, j // 4]
        across = jnp.where(lane == j, value, across)
        down = jnp.where(sub == j, value, down)
    earlier = jnp.where((across == down) & (sub < lane), 1.0, 0.0)
    rank = jnp.sum(earlier, axis=0, keepdims=True)
    slot_row = across[:1].astype(f32) * 2.0 + rank
    slot_buf[me] = jnp.broadcast_to(slot_row, (8, 128))

    def slot_copy(n):
        return remote(
            slot_buf.at[me], slot_buf.at[me], slot_send.at[n], slot_recv.at[me],
            (sec, exclusive(me, peers - n, peers)),
        )

    lanes = iota((rows, 128), 1)

    def project(values):
        h_ref[...] = values
        scaled = (values * gain[...]).astype(bf16)
        squares = jnp.sum(values * values, axis=1, keepdims=True)
        high = squares.astype(bf16).astype(f32)
        third[...] = jnp.where(lanes == 32, high, jnp.where(lanes == 33, squares - high, 0.0))
        third[:, :32] = lax.dot_general(scaled, state_w[0], across_last, preferred_element_type=f32)
        low = jnp.dot(scaled, dt_in[0], preferred_element_type=f32)
        part[:, :256] = low.astype(bf16)
        part[:, 256:] = third[...].astype(bf16)

    project(inputs[...].reshape(rows, chans).astype(f32))
    pl.semaphore_wait(barrier, total - 1)

    @pl.when(sec == 1)
    def _():
        remote(own, relay, relay_send, relay_recv, partner).wait_recv()
        project(relay[...].astype(f32))

    h = h_ref[...]

    reducer = lax.rem(me, 2) == 0
    share = me // 2

    def rs_to(n):
        return exclusive(share, lax.rem(chips - n, chips), chips)

    def rs_copy(n):
        at = pl.multiple_of(rs_to(n) * 16, 16)
        return remote(
            part.at[pl.ds(at, 16)], rs_buf.at[me], rs_send.at[n], rs_recv.at[me],
            (sec, 2 * rs_to(n)),
        )

    @pl.when(jnp.logical_not(reducer))
    def _():
        rs_copy(0).start()

    loop(1, chips, lambda n: rs_copy(n).start())

    share_at = pl.multiple_of(share * 16, 16)

    def ag_copy(n):
        return remote(
            summed, ag_buf.at[pl.ds(share_at, 16)], ag_send.at[n], ag_recv.at[share],
            (sec, exclusive(me, peers - n, peers)),
        )

    def rs_arrived(source):
        return remote(part.at[pl.ds(0, 16)], rs_buf.at[source], rs_send.at[0], rs_recv.at[source], (sec, me))

    @pl.when(reducer)
    def _():
        rs_buf[me] = part[pl.ds(share_at, 16), :]
        loop(1, peers, lambda n: rs_arrived(exclusive(me, peers - n, peers)).wait_recv())
        whole = jnp.sum(rs_buf[...].astype(f32), axis=0)
        square = whole[:, 288:289] + whole[:, 289:290]
        scale = lax.rsqrt(square / full + 1e-05)
        scale_high = scale.astype(bf16).astype(f32)
        lane3 = iota((16, WIDE), 1)
        result = jnp.where(
            lane3 == 288, scale_high, jnp.where(lane3 == 289, scale - scale_high, whole * scale)
        )
        summed[...] = result.astype(bf16)
        ag_buf[pl.ds(share_at, 16), :] = summed[...]
        loop(1, peers, lambda n: ag_copy(n).start())

    loop(1, peers, lambda n: slot_copy(n).start())

    def ag_arrived(chip):
        at = pl.multiple_of(chip * 16, 16)
        return remote(summed, ag_buf.at[pl.ds(at, 16)], ag_send.at[0], ag_recv.at[chip], (sec, me))

    @pl.when(jnp.logical_not(reducer))
    def _():
        ag_arrived(share).wait_recv()

    loop(1, chips, lambda n: ag_arrived(rs_to(n)).wait_recv())

    tail = ag_buf[:, 256:]
    tail_f = tail.astype(f32)
    scale = tail_f[:, 32:33] + tail_f[:, 33:34]
    u = (scaled_of(h, scale, gain[...])).astype(bf16).astype(f32)
    step_pre = jnp.dot(ag_buf[:, :256], dt_out[0], preferred_element_type=f32) + bias[...]
    step_dt = jnp.maximum(step_pre, 0.0) + jnp.log1p(jnp.exp(-jnp.abs(step_pre)))
    step_ref[...] = step_dt
    du_ref[...] = step_dt * u
    spread = jnp.where(iota((rows * 16, rows), 0) >> 4 == iota((rows * 16, rows), 1), 1.0, 0.0)
    repeated = jnp.dot(spread.astype(bf16), tail, preferred_element_type=f32)
    state_lane = iota((rows * 16, 128), 1)
    state_row = iota((rows * 16, 128), 0) & 15
    ones = jnp.ones((128, 128), bf16)
    b_ref[...] = jnp.dot(
        jnp.where(state_lane == state_row, repeated, 0.0).astype(bf16), ones,
        preferred_element_type=f32,
    )
    c_ref[...] = jnp.dot(
        jnp.where(state_lane == state_row + 16, repeated, 0.0).astype(bf16), ones,
        preferred_element_type=f32,
    )
    negative = -rate[0]

    def advance(t, states):
        after = []
        for m in range(batches):
            row = m * seq + t
            at = pl.multiple_of(row * 16, 16)
            b_in, c_out = b_ref[pl.ds(at, 16), :], c_ref[pl.ds(at, 16), :]
            b_in = jnp.concatenate([b_in] * (chans // 128), axis=1)
            c_out = jnp.concatenate([c_out] * (chans // 128), axis=1)
            state = (
                jnp.exp(step_ref[pl.ds(row, 1), :] * negative) * states[m]
                + du_ref[pl.ds(row, 1), :] * b_in
            )
            mixed_ref[pl.ds(row, 1), :] = jnp.sum(state * c_out, axis=0, keepdims=True)
            after.append(state)
        return tuple(after)

    lax.fori_loop(
        0, seq, advance, tuple(jnp.zeros((16, chans), f32) for _ in range(batches)), unroll=4
    )
    mixed = mixed_ref[...] + skip[...] * u
    own[...] = (h + mixed * (u / (1.0 + jnp.exp(-u)))).astype(bf16)
    relay_copy = remote(own, relay, relay_send, relay_recv, partner)
    relay_copy.start()

    def slot_arrived(n):
        source = exclusive(me, peers - n, peers)
        remote(
            slot_buf.at[source], slot_buf.at[source], slot_send.at[0], slot_recv.at[source], (sec, me)
        ).wait_recv()

    loop(1, peers, slot_arrived)
    slot_table = jnp.concatenate([slot_buf[n, :1, :] for n in range(peers)], axis=0).astype(bf16)
    token = iota((1, 128), 1)
    position, batch = token & (seq - 1), token // seq
    j_row, token_at = iota((128, 128), 0), iota((128, 128), 1)
    flat_first = ((token_at & 3) * 2 + token_at // seq) * 2
    block_mask = iota((peers, 128), 0) == (iota((peers, 128), 1) & (seq - 1)) >> 2
    slots = []
    for k in range(2):
        pick = jnp.where(j_row == flat_first + k, 1.0, 0.0).astype(bf16)
        picked = jnp.dot(slot_table, pick, preferred_element_type=f32)
        slots.append(jnp.sum(jnp.where(block_mask, picked, 0.0), axis=0, keepdims=True))

    def placed(count, expert):
        q, r = iota((count, 128), 0), iota((count, 128), 1)
        wanted = ((expert + (q >> 5)) * 2 + (q & 1)).astype(f32)
        same = ((q >> 1) & (peers - 1)) == (r & (seq - 1)) >> 2
        return same & ((slots[0] == wanted) | (slots[1] == wanted))

    place_all = jnp.where(placed(16 * peers, 0), 1.0, 0.0).astype(bf16)
    q, r = iota((rows, rows), 0), iota((rows, rows), 1)
    regroup = jnp.where(
        r == ((q >> 2) & 1) * seq + (q >> 3) * 4 + (q & 3), 1.0, 0.0
    ).astype(bf16)

    @pl.when(sec == 0)
    def _():
        relay_copy.wait_recv()

    final = jnp.where(sec == 0, relay[...].astype(f32), own[...].astype(f32))
    own_at = pl.multiple_of(me * chans, chans)
    final_scaled = (final * moe_gain[:, pl.ds(own_at, chans)]).astype(bf16)
    squares = jnp.sum(final * final, axis=1, keepdims=True)
    third[...] = jnp.where(lanes == 8, squares, 0.0)
    third[:, :8] = lax.dot_general(
        final_scaled, router[:, pl.ds(own_at, chans)], across_last, preferred_element_type=f32
    )
    stat_buf[me] = jnp.transpose(third[...])[:16]

    def stat_copy(n):
        return remote(
            stat_buf.at[me], stat_buf.at[me], stat_send.at[n], stat_recv.at[me],
            (sec, exclusive(me, peers - n, peers)),
        )

    xsend[...] = jnp.dot(place_all, final_scaled, preferred_element_type=f32).astype(bf16)
    rsend[...] = jnp.dot(regroup, final.astype(bf16), preferred_element_type=f32)
    to_section = me // chips
    column = pl.multiple_of(lax.rem(me, chips) * chans, chans)

    def x_copy(n):
        chip = exclusive(me // 2, lax.rem(chips - n, chips), chips)
        at = pl.multiple_of(chip * 32, 32)
        return remote(
            xsend.at[pl.ds(at, 32)], xrow.at[:, pl.ds(column, chans)], x_send.at[n],
            x_recv.at[lax.rem(me, chips)], (to_section, chip * 2 + sec),
        )

    def r_copy(n):
        block = exclusive(me // 2, lax.rem(chips - n, chips), chips) * 2 + sec
        at = pl.multiple_of(block * 8, 8)
        return remote(
            rsend.at[pl.ds(at, 8)], resid.at[:, pl.ds(column, chans)], r_send.at[n],
            r_recv.at[lax.rem(me, chips)], (to_section, block),
        )

    itself = (to_section == sec) & (lax.rem(me, 2) == sec)

    @pl.when(itself)
    def _():
        xrow[:, pl.ds(column, chans)] = xsend[pl.ds(pl.multiple_of(me // 2 * 32, 32), 32), :]
        resid[:, pl.ds(column, chans)] = rsend[pl.ds(pl.multiple_of(me * 8, 8), 8), :]

    @pl.when(jnp.logical_not(itself))
    def _():
        x_copy(0).start()

    loop(1, chips, lambda n: x_copy(n).start())
    loop(1, peers, lambda n: stat_copy(n).start())

    @pl.when(jnp.logical_not(itself))
    def _():
        r_copy(0).start()

    loop(1, chips, lambda n: r_copy(n).start())

    def x_arrived(j):
        @pl.when(jnp.logical_not(itself & (j == lax.rem(me, chips))))
        def _():
            at = pl.multiple_of(j * chans, chans)
            remote(
                xsend.at[pl.ds(0, 32)], xrow.at[:, pl.ds(at, chans)], x_send.at[0], x_recv.at[j],
                (sec, me),
            ).wait_recv()

    def r_arrived(j):
        @pl.when(jnp.logical_not(itself & (j == lax.rem(me, chips))))
        def _():
            at = pl.multiple_of(j * chans, chans)
            remote(
                rsend.at[pl.ds(0, 8)], resid.at[:, pl.ds(at, chans)], r_send.at[0], r_recv.at[j],
                (sec, me),
            ).wait_recv()

    def stat_arrived(n):
        source = exclusive(me, peers - n, peers)
        remote(
            stat_buf.at[source], stat_buf.at[source], stat_send.at[0], stat_recv.at[source], (sec, me)
        ).wait_recv()

    loop(1, peers, stat_arrived)
    stats = jnp.sum(stat_buf[...], axis=0)
    token_scale = lax.rsqrt(stats[8:9] / full + 1e-05)
    logits = stats[:8] * token_scale
    exps = jnp.exp(logits - jnp.max(logits, axis=0, keepdims=True))
    probs = exps / jnp.sum(exps, axis=0, keepdims=True)
    expert_row = iota((8, 128), 0)
    chosen = [
        jnp.sum(
            jnp.where(expert_row == slots[k].astype(jnp.int32) >> 1, probs, 0.0),
            axis=0, keepdims=True,
        )
        for k in range(2)
    ]
    both = chosen[0] + chosen[1]
    weights = [chosen[k] / both for k in range(2)]
    row_scale = jnp.sum(
        jnp.where(placed(32, me // 2), token_scale, 0.0), axis=1, keepdims=True
    )
    loop(0, chips, x_arrived)

    def part_copy(n):
        return remote(parts.at[n], theirs.at[n], p_send.at[n], p_recv.at[n], partner)

    def first_matmuls(n):
        slot = lax.rem(n, IN_SLOTS)
        in_copy(n).wait()
        for g in range(2):
            product = jnp.dot(xrow[...], win[slot, g], preferred_element_type=f32)
            parts[n, g] = (product * row_scale).astype(bf16)

        @pl.when(n < half)
        def _():
            part_copy(n).start()

        @pl.when(n + IN_SLOTS < steps)
        def _():
            in_copy(n + IN_SLOTS).start()

    loop(0, steps, first_matmuls)

    def unit_copy(k):
        return remote(units.at[k], units.at[half + k], u_send.at[k], u_recv.at[k], partner)

    def down_matmul(n):
        slot = lax.rem(n, OUT_SLOTS)
        out_copy(n).wait()
        acc[...] += jnp.dot(units[n], wout[slot], preferred_element_type=f32)

        @pl.when(n + OUT_SLOTS < steps)
        def _():
            out_copy(n + OUT_SLOTS).start()

    acc[...] = jnp.zeros_like(acc)

    def own_units(k):
        part_copy(k).wait_recv()
        gate = parts[half + k, 0].astype(f32) + theirs[k, 0].astype(f32)
        up = parts[half + k, 1].astype(f32) + theirs[k, 1].astype(f32)
        units[k] = (gate / (1.0 + jnp.exp(-gate)) * up).astype(bf16)
        unit_copy(k).start()
        down_matmul(k)

    loop(0, half, own_units)

    def other_units(k):
        unit_copy(k).wait_recv()
        down_matmul(half + k)

    loop(0, half, other_units)

    pieces = acc.shape[1] // chans
    stacked = jnp.concatenate(
        [acc[:, f * chans:(f + 1) * chans] for f in range(pieces)], axis=0
    ).astype(bf16)
    count = 32 * pieces
    q, z = iota((count, count), 0), iota((count, count), 1)
    order = jnp.where(
        z == (q & 7) * 32 + (q >> 4) * 2 + ((q >> 3) & 1), 1.0, 0.0
    ).astype(bf16)
    ret[...] = jnp.dot(order, stacked, preferred_element_type=f32).astype(bf16)

    def back_copy(n):
        block = exclusive(me, peers - n, peers)
        to = pl.multiple_of(block * 16, 16)
        at = pl.multiple_of(me * 16, 16)
        return remote(
            ret.at[pl.ds(to, 16)], back.at[pl.ds(at, 16)], b_send.at[n], b_recv.at[me], (sec, block)
        )

    loop(1, peers, lambda n: back_copy(n).start())
    mine_at = pl.multiple_of(me * 16, 16)
    back[pl.ds(mine_at, 16), :] = ret[pl.ds(mine_at, 16), :]

    tok, lane64 = iota((64, 128), 0) & 7, iota((64, 128), 1)
    here = lane64 == (tok >> 2) * seq + me * 4 + (tok & 3)
    mix_row, mix_lane = iota((64, 256), 0), iota((64, 256), 1)
    slot_of = ((mix_lane >> 5) * 2 + ((mix_lane >> 3) & 1)).astype(f32)
    aligned = (mix_row >> 3) == (mix_lane & 7)
    mix = jnp.zeros((64, 256), f32)
    for k in range(2):
        weight = jnp.sum(jnp.where(here, weights[k], 0.0), axis=1, keepdims=True)
        slot = jnp.sum(jnp.where(here, slots[k], 0.0), axis=1, keepdims=True)
        mix = mix + jnp.where(aligned & (slot == slot_of), weight, 0.0)
    mix_high = mix.astype(bf16)
    mix_low = (mix - mix_high.astype(f32)).astype(bf16)
    loop(0, chips, r_arrived)

    def back_arrived(n):
        source = exclusive(me, peers - n, peers)
        at = pl.multiple_of(source * 16, 16)
        remote(
            ret.at[pl.ds(0, 16)], back.at[pl.ds(at, 16)], b_send.at[0], b_recv.at[source], (sec, me)
        ).wait_recv()

    loop(1, peers, back_arrived)
    routed = jnp.dot(mix_high, back[...], preferred_element_type=f32) + jnp.dot(
        mix_low, back[...], preferred_element_type=f32
    )
    for f in range(pieces):
        columns = slice(f * chans, (f + 1) * chans)
        value = (resid[:, columns] + routed[f * 8:(f + 1) * 8]).astype(bf16)
        out[0, :, columns] = value[:4]
        out[1, :, columns] = value[4:]

    @pl.when(jnp.logical_not(reducer))
    def _():
        rs_copy(0).wait_send()

    loop(1, chips, lambda n: rs_copy(n).wait_send())

    @pl.when(reducer)
    def _():
        loop(1, peers, lambda n: ag_copy(n).wait_send())

    @pl.when(jnp.logical_not(itself))
    def _():
        x_copy(0).wait_send()
        r_copy(0).wait_send()

    def x_left(n):
        x_copy(n).wait_send()
        r_copy(n).wait_send()

    loop(1, chips, x_left)

    def rest_left(n):
        slot_copy(n).wait_send()
        stat_copy(n).wait_send()
        back_copy(n).wait_send()

    loop(1, peers, rest_left)

    def halves_left(k):
        part_copy(k).wait_send()
        unit_copy(k).wait_send()

    loop(0, half, halves_left)
    relay_copy.wait_send()


def exclusive(a, b, count):
    total, bit = 0, 1
    while bit < count:
        total = total + lax.rem(a // bit + b // bit, 2) * bit
        bit *= 2
    return total


def scaled_of(h, scale, gain):
    return h * scale * gain


def fused(
    inputs, expert_ids, mamba_gain, dt_in, dt_out, dt_bias, state_in, decay_rate, skip_gain,
    moe_gain, router, expert_in, expert_out,
):
    f32, bf16 = jnp.float32, jnp.bfloat16
    peers = lax.axis_size("expert")
    batches, seq, chans = inputs.shape
    rows = batches * seq
    depth, columns = expert_in.shape[1:]
    steps = columns // STEP_COLUMNS
    half = steps // 2
    chips = peers // 2
    vmem = pl.BlockSpec(memory_space=pltpu.VMEM)
    smem = pl.BlockSpec(memory_space=pltpu.SMEM)
    hbm = pl.BlockSpec(memory_space=pl.ANY)
    dma = pltpu.SemaphoreType.DMA
    scratch = [
        pltpu.VMEM((IN_SLOTS, 2, depth, STEP_COLUMNS), bf16),
        pltpu.VMEM((OUT_SLOTS, STEP_COLUMNS, depth), bf16),
        pltpu.VMEM((rows, WIDE), bf16),
        pltpu.VMEM((peers, 16, WIDE), bf16),
        pltpu.VMEM((16, WIDE), bf16),
        pltpu.VMEM((rows, WIDE), bf16),
        pltpu.VMEM((rows, 128), f32),
        pltpu.VMEM((rows, chans), f32),
        pltpu.VMEM((rows, chans), f32),
        pltpu.VMEM((rows, chans), f32),
        pltpu.VMEM((rows, chans), f32),
        pltpu.VMEM((rows * 16, 128), f32),
        pltpu.VMEM((rows * 16, 128), f32),
        pltpu.VMEM((rows, chans), bf16),
        pltpu.VMEM((rows, chans), bf16),
        pltpu.VMEM((peers, 8, 128), f32),
        pltpu.VMEM((peers, 16, 128), f32),
        pltpu.VMEM((16 * peers, chans), bf16),
        pltpu.VMEM((32, depth), bf16),
        pltpu.VMEM((rows, chans), f32),
        pltpu.VMEM((8, depth), f32),
        pltpu.VMEM((steps, 2, 32, STEP_COLUMNS), bf16),
        pltpu.VMEM((half, 2, 32, STEP_COLUMNS), bf16),
        pltpu.VMEM((steps, 32, STEP_COLUMNS), bf16),
        pltpu.VMEM((32, depth), f32),
        pltpu.VMEM((16 * peers, chans), bf16),
        pltpu.VMEM((16 * peers, chans), bf16),
        dma((IN_SLOTS,)), dma((OUT_SLOTS,)),
        dma((chips,)), dma((peers,)), dma((peers,)), dma((chips,)), dma, dma,
        dma((peers,)), dma((peers,)), dma((peers,)), dma((peers,)),
        dma((chips,)), dma((chips,)), dma((chips,)), dma((chips,)),
        dma((half,)), dma((half,)), dma((half,)), dma((half,)),
        dma((peers,)), dma((peers,)),
    ]
    return pl.pallas_call(
        kernel,
        out_shape=jax.ShapeDtypeStruct((batches, seq // peers, depth), bf16),
        in_specs=[vmem, smem] + [vmem] * 9 + [hbm, hbm],
        out_specs=vmem,
        scratch_shapes=scratch,
        compiler_params=pltpu.CompilerParams(
            collective_id=0, has_side_effects=True, vmem_limit_bytes=62 << 20
        ),
    )(
        inputs, expert_ids.transpose(1, 2, 0), mamba_gain, dt_in, dt_out, dt_bias,
        state_in.transpose(0, 2, 1), decay_rate.transpose(0, 2, 1), skip_gain,
        moe_gain.reshape(1, -1), router.T, expert_in, expert_out,
    )


def fits(mesh):
    return mesh.shape["section"] == 2 and mesh.shape["expert"] == 16


def solution(mesh):
    placed = (
        P(None, None, "expert"),
        P("expert", None, None),
        P("section", "expert"),
        P("section", "expert", None),
        P("section", None, "expert"),
        P("section", "expert"),
        P("section", "expert", None),
        P("section", "expert", None),
        P("section", "expert"),
        P(),
        P(),
        P(None, "section", "expert"),
        P("expert", "section"),
    )
    body = fused if fits(mesh) else shards
    return jax.shard_map(
        body, mesh=mesh, in_specs=placed, out_specs=P(None, "expert", "section"), check_vma=False
    )
```
